128 devices in a mesh: expert: 16 (over x, y), row: 8 (over z, core).
Axes of the slice: x: 4, y: 4, z: 4, core: 2. Of those that a mesh axis runs over, the one named last changes fastest.
Arguments:
- weights: bfloat16 [64, 7168, 2048], P('expert', 'row'), may hold values from -0.0625 to 0.0625
- prev_rows: float32 [7168, 512], P('row'), may hold values from -6 to 6
- prev_cols: float32 [2048, 256], replicated, may hold values from -6 to 6
Outputs:
- row_basis: float32 [7168, 512], P('row')
- col_basis: float32 [2048, 256], replicated
The draws below stay inside these ranges and needn't reach their ends.
All inputs are finite; a program needn't handle non-finite values.
Results may differ from the reference program's by a relative error of at most 0.004.
Values sent between devices are 32-bit elements; how exact they have to be, the bound alone decides.
A program may use at most 128 MiB of HBM per device.

```python
import math
import jax
import jax.numpy as jnp
from jax import lax

D = 7168
F = 2048
R1 = 512
R2 = 256
EXPERTS = 64


def block_levels(own_key, extent, pieces, smallest, largest):
    def one(dim, blocks):
        draws = jax.random.uniform(jax.random.fold_in(jax.random.fold_in(own_key, 6), dim), (blocks,), jnp.float32, smallest / len(pieces), largest / len(pieces))
        return jnp.repeat(jnp.exp(draws), extent[dim] // blocks).reshape((-1,) + (1,) * (len(extent) - dim - 1))

    gain = one(*pieces[0])
    for cut in pieces[1:]:
        gain = gain * one(*cut)
    return gain


def gaussian(key, extent, deviation, bound, pieces=(), held_as=jnp.bfloat16):
    factor_of = block_levels(key, extent, pieces, -0.22, 0.18) if pieces else 1.0
    drawn = jax.random.normal(key, extent, jnp.float32) * deviation * factor_of
    return jnp.minimum(jnp.maximum(drawn, -bound), bound).astype(held_as)


def setup_inputs(seed: int = 0) -> dict:
    splits = jax.random.split(jax.random.key(seed), 4)
    weights = gaussian(splits[0], (EXPERTS, D, F), D ** -0.5, 0.0625, ((0, 16), (1, 8)))
    prev_rows = gaussian(splits[1], (D, R1), 1.0, 6.0, ((0, 8),), jnp.float32)
    prev_cols = gaussian(splits[2], (F, R2), 1.0, 6.0, (), jnp.float32)
    return {"weights": weights, "prev_rows": prev_rows, "prev_cols": prev_cols}


def reference(weights, prev_rows, prev_cols):
    highest = lax.Precision.HIGHEST
    cols_low = prev_cols.astype(jnp.bfloat16)

    def first(total, matrix):
        proj = jnp.dot(matrix.astype(jnp.float32), cols_low.astype(jnp.float32), preferred_element_type=jnp.float32)
        core = jnp.dot(prev_rows.T, proj, precision=highest)
        return (total + jnp.dot(proj, core.T, precision=highest), None)
    images, _ = lax.scan(first, jnp.zeros((D, R1), jnp.float32), weights)
    row_gram = jnp.dot(images.T, images, precision=highest)
    row_factor = jnp.linalg.cholesky(row_gram)
    row_basis = math.sqrt(D) * jax.scipy.linalg.solve_triangular(row_factor, images.T, lower=True).T

    def second(total, matrix):
        proj = jnp.dot(matrix.astype(jnp.float32), cols_low.astype(jnp.float32), preferred_element_type=jnp.float32)
        core_two = jnp.dot(row_basis.T, proj, precision=highest)
        back = jnp.dot(row_basis, core_two, precision=highest).astype(jnp.bfloat16)
        return (total + jnp.dot(matrix.T.astype(jnp.float32), back.astype(jnp.float32), preferred_element_type=jnp.float32), None)
    colimg, _ = lax.scan(second, jnp.zeros((F, R2), jnp.float32), weights)
    col_gram = jnp.dot(colimg.T, colimg, precision=highest)
    col_factor = jnp.linalg.cholesky(col_gram)
    col_basis = math.sqrt(F) * jax.scipy.linalg.solve_triangular(col_factor, colimg.T, lower=True).T
    return (row_basis, col_basis)
```

```python
import functools
import math

import jax
import jax.numpy as jnp
from jax import lax
from jax.experimental import pallas as pl
from jax.experimental.pallas import tpu as pltpu
from jax.sharding import PartitionSpec as P

D = 7168
F = 2048
R1 = 512
R2 = 256
ROWS = 896
LOCAL = 4
MESH = pl.DeviceIdType.MESH
HIGHEST = lax.Precision.HIGHEST
F32 = jnp.float32
BF16 = jnp.bfloat16


def dot(a, b, ca, cb, precision=None):
    return lax.dot_general(
        a, b, (((ca,), (cb,)), ((), ())), precision=precision, preferred_element_type=F32
    )


def split(value):
    high = value.astype(BF16)
    return high, (value - high.astype(F32)).astype(BF16)


def dot3(ah, al, bh, bl, ca, cb):
    return dot(ah, bh, ca, cb) + (dot(ah, bl, ca, cb) + dot(al, bh, ca, cb))


def lane_of(block, j):
    return jnp.broadcast_to(block[:, j : j + 1], (8, 128))


def row_of(block, k):
    return jnp.broadcast_to(block[k : k + 1, :], (8, 128))


def inverse_factor_of_tile(blocks):
    count = 16
    sub = lax.broadcasted_iota(jnp.int32, (8, 128), 0)
    lane = lax.broadcasted_iota(jnp.int32, (8, 128), 1)
    left = list(blocks)
    right = [jnp.where(lane == sub + 8 * b, 1.0, 0.0).astype(F32) for b in range(count)]
    for b in range(count):
        columns = [lane_of(left[b], 8 * b + j) for j in range(8)]
        corner = {(k, j): row_of(columns[j], k) for j in range(8) for k in range(j, 8)}
        last = b == count - 1
        lrows = None if last else [row_of(left[b], k) for k in range(8)]
        rrows = [row_of(right[b], k) for k in range(8)]
        roots, low = [], {}
        for i in range(8):
            root = lax.rsqrt(corner[i, i])
            roots.append(root)
            for k in range(i + 1, 8):
                low[k, i] = corner[k, i] * root
            for j in range(i + 1, 8):
                for k in range(j, 8):
                    corner[k, j] = corner[k, j] - low[k, i] * low[j, i]
            rrows[i] = rrows[i] * root
            for k in range(i + 1, 8):
                rrows[k] = rrows[k] - low[k, i] * rrows[i]
            if not last:
                lrows[i] = lrows[i] * root
                for k in range(i + 1, 8):
                    lrows[k] = lrows[k] - low[k, i] * lrows[i]
        whole = rrows[7]
        for i in range(6, -1, -1):
            whole = jnp.where(sub == i, rrows[i], whole)
        right[b] = whole
        for t in range(b + 1, count):
            q = [lane_of(left[t], 8 * b + j) for j in range(8)]
            lt, rt = left[t], right[t]
            for i in range(8):
                term = q[i] * roots[i]
                for k in range(i + 1, 8):
                    q[k] = q[k] - low[k, i] * term
                lt = lt - term * lrows[i]
                rt = rt - term * rrows[i]
            left[t], right[t] = lt, rt
    return right


def inverse_factor(n, gram, inverse, between=None):
    tiles = n // 128
    inverse[...] = jnp.zeros_like(inverse)

    def step(k, carry):
        o = pl.multiple_of(k * 128, 128)
        rows = inverse_factor_of_tile(
            [gram[pl.ds(o + 8 * b, 8), pl.ds(o, 128)] for b in range(16)]
        )
        inverse[pl.ds(o, 128), pl.ds(o, 128)] = jnp.concatenate(rows, axis=0)
        for kk in range(tiles):

            @pl.when(k == kk)
            def _():
                a, z = 128 * kk, 128 * kk + 128
                own = inverse[a:z, a:z]
                if kk > 0:
                    inverse[a:z, 0:a] = dot(own, inverse[a:z, 0:a], 1, 0, HIGHEST)
                if kk < tiles - 1:
                    upper = dot(own, gram[a:z, z:n], 1, 0, HIGHEST)
                    gram[z:n, z:n] = gram[z:n, z:n] - dot(upper, upper, 0, 0, HIGHEST)
                    inverse[z:n, 0:z] = inverse[z:n, 0:z] - dot(
                        upper, inverse[a:z, 0:z], 0, 0, HIGHEST
                    )
                if between is not None:
                    between(kk)

        return carry

    lax.fori_loop(0, tiles, step, 0)


class Place:
    def __init__(self):
        expert, row = lax.axis_index("expert"), lax.axis_index("row")
        self.at = {
            "x": lax.div(expert, 4), "y": lax.rem(expert, 4),
            "z": lax.div(row, 2), "c": lax.rem(row, 2),
        }

    def index(self, axis, d):
        return lax.rem(self.at[axis] + d, 4)

    def peer(self, axis, d):
        at = dict(self.at)
        at[axis] = lax.rem(at[axis] + d, 2 if axis == "c" else 4)
        return (at["x"] * 4 + at["y"], at["z"] * 2 + at["c"])


class Sender:
    def __init__(self, place, send_sem, recv_sem):
        self.place, self.send_sem, self.recv_sem, self.used = place, send_sem, recv_sem, 0

    def copy(self, source, target, axis, d):
        n = self.used
        self.used += 1
        return pltpu.make_async_remote_copy(
            src_ref=source, dst_ref=target, send_sem=self.send_sem.at[n],
            recv_sem=self.recv_sem.at[n], device_id=self.place.peer(axis, d), device_id_type=MESH,
        )


class RowSum:
    def __init__(self, sender, rows, part, sibling, arrived, full):
        place = sender.place
        c = place.at["c"]
        half, chunk = rows // 2, rows // 8
        self.half, self.chunk, self.c = half, chunk, c
        self.part, self.sibling, self.arrived, self.full = part, sibling, arrived, full
        self.base = c * half
        other = (1 - c) * half
        self.place = place
        self.swap = sender.copy(part.at[pl.ds(other, half)], sibling, "c", 1)
        self.spread = [
            sender.copy(
                part.at[pl.ds(self.base + place.index("z", d) * chunk, chunk)],
                arrived.at[d - 1], "z", d,
            )
            for d in (1, 2, 3)
        ]
        self.mine = self.base + place.at["z"] * chunk
        own = full.at[pl.ds(self.mine, chunk)]
        self.gather = [sender.copy(own, own, "z", d) for d in (1, 2, 3)]
        self.across = [sender.copy(own, own, "c", 1)]
        for d in (1, 2, 3):
            got = full.at[pl.ds(self.base + place.index("z", 4 - d) * chunk, chunk)]
            self.across.append(sender.copy(got, got, "c", 1))

    def start(self):
        self.swap.start()

    def scatter(self):
        self.swap.wait_recv()
        for d in (1, 2, 3, 0):
            p = self.place.index("z", d)
            there = pl.ds(self.base + p * self.chunk, self.chunk)
            self.part[there] = self.part[there] + self.sibling[pl.ds(p * self.chunk, self.chunk)]
            if d:
                self.spread[d - 1].start()

    def reduce(self):
        for copy in self.spread:
            copy.wait_recv()
        there = pl.ds(self.mine, self.chunk)
        self.full[there] = (self.part[there] + self.arrived[0]) + (
            self.arrived[1] + self.arrived[2]
        )
        for copy in self.gather:
            copy.start()
        self.across[0].start()

    def forward(self):
        for d in (1, 2, 3):
            self.gather[d - 1].wait_recv()
            self.across[d].start()

    def finish(self):
        for copy in self.across:
            copy.wait()
        self.swap.wait_send()
        for copy in self.spread + self.gather:
            copy.wait_send()


class PlaneSum:
    def __init__(self, sender, first, second, part, arrived1, half, arrived2, full):
        place = sender.place
        m1, m2 = place.at[first], place.at[second]
        self.part, self.arrived1, self.half = part, arrived1, half
        self.arrived2, self.full, self.m1, self.m2 = arrived2, full, m1, m2
        self.one = [
            sender.copy(
                part.at[pl.ds(place.index(first, d) * 224, 224)], arrived1.at[d - 1], first, d
            )
            for d in (1, 2, 3)
        ]
        self.two = [
            sender.copy(
                half.at[pl.ds(place.index(second, d) * 56, 56)], arrived2.at[d - 1], second, d
            )
            for d in (1, 2, 3)
        ]
        own = full.at[pl.ds(m1 * 224 + m2 * 56, 56)]
        self.three = [sender.copy(own, own, second, d) for d in (1, 2, 3)]
        wide = full.at[pl.ds(m1 * 224, 224)]
        self.four = [sender.copy(wide, wide, first, d) for d in (1, 2, 3)]

    def start(self):
        for copy in self.one:
            copy.start()

    def reduce1(self):
        for copy in self.one:
            copy.wait_recv()
        a = self.arrived1
        self.half[...] = (self.part[pl.ds(self.m1 * 224, 224)] + a[0]) + (a[1] + a[2])
        for copy in self.two:
            copy.start()

    def reduce2(self):
        for copy in self.two:
            copy.wait_recv()
        a = self.arrived2
        self.full[pl.ds(self.m1 * 224 + self.m2 * 56, 56)] = (
            self.half[pl.ds(self.m2 * 56, 56)] + a[0]
        ) + (a[1] + a[2])
        for copy in self.three:
            copy.start()

    def gather(self):
        for copy in self.three:
            copy.wait_recv()
        for copy in self.four:
            copy.start()

    def finish(self):
        for copy in self.four:
            copy.wait_recv()
        for copy in self.one + self.two + self.three + self.four:
            copy.wait_send()


class CubeSum:
    def __init__(self, sender, axes, u0, n, part, arrived1, sum1, arrived2, sum2, arrived3, full):
        place = sender.place
        a1, a2, a3 = axes
        m1, m2, m3 = (place.at[a] for a in axes)
        base = place.at["c"] * 8 + u0
        slabs = pl.ds(u0, n)
        self.slabs, self.m1, self.m2, self.m3, self.base, self.n = slabs, m1, m2, m3, base, n
        self.part, self.arrived1, self.sum1 = part, arrived1, sum1
        self.arrived2, self.sum2, self.arrived3, self.full = arrived2, sum2, arrived3, full
        self.one = [
            sender.copy(
                part.at[pl.ds(base, n), pl.ds(place.index(a1, d) * 64, 64)],
                arrived1.at[d - 1, slabs], a1, d,
            )
            for d in (1, 2, 3)
        ]
        self.two = [
            sender.copy(
                sum1.at[slabs, pl.ds(place.index(a2, d) * 16, 16)],
                arrived2.at[d - 1, slabs], a2, d,
            )
            for d in (1, 2, 3)
        ]
        self.three = [
            sender.copy(arrived3.at[m3, slabs], arrived3.at[m3, slabs], a3, d) for d in (1, 2, 3)
        ]
        own = full.at[pl.ds(base, n), pl.ds(m1 * 64 + m2 * 16, 16)]
        self.four = [sender.copy(own, own, a2, d) for d in (1, 2, 3)]
        wide = full.at[pl.ds(base, n), pl.ds(m1 * 64, 64)]
        self.five = [sender.copy(wide, wide, a1, d) for d in (1, 2, 3)]
        whole = full.at[pl.ds(base, n)]
        self.six = sender.copy(whole, whole, "c", 1)

    def start(self):
        for copy in self.one:
            copy.start()

    def reduce1(self):
        for copy in self.one:
            copy.wait_recv()
        a, s = self.arrived1, self.slabs
        own = self.part[pl.ds(self.base, self.n), pl.ds(self.m1 * 64, 64)]
        self.sum1[s] = (own + a[0, s]) + (a[1, s] + a[2, s])
        for copy in self.two:
            copy.start()

    def reduce2(self):
        for copy in self.two:
            copy.wait_recv()
        a, s = self.arrived2, self.slabs
        own = self.sum1[s, pl.ds(self.m2 * 16, 16)]
        self.arrived3[self.m3, s] = (own + a[0, s]) + (a[1, s] + a[2, s])
        for copy in self.three:
            copy.start()

    def reduce3(self):
        for copy in self.three:
            copy.wait()
        a, s = self.arrived3, self.slabs
        self.full[pl.ds(self.base, self.n), pl.ds(self.m1 * 64 + self.m2 * 16, 16)] = (
            a[0, s] + a[1, s]
        ) + (a[2, s] + a[3, s])
        for copy in self.four:
            copy.start()

    def gather(self):
        for copy in self.four:
            copy.wait_recv()
        for copy in self.five:
            copy.start()

    def across(self):
        for copy in self.five:
            copy.wait_recv()
        self.six.start()

    def finish(self):
        self.six.wait()
        for copy in self.one + self.two + self.four + self.five:
            copy.wait_send()


def kernel(
    w_hbm, x_hbm, c_hbm, rb_hbm, cb_hbm,
    w, ph, pw, pth, ptw, xh, xw, cols, pf,
    cp, csib, carr, cfull, ch, cw,
    ip, iarr1, ihalf, iarr2, imf,
    gp, gsib, garr, gfull, gram, inv, vh, vw, th, tw,
    rb, dp, dsib, darr1, dsum1, darr2, dsum2, darr3, df,
    local_sem, send_sem, recv_sem,
):
    place = Place()
    c = place.at["c"]
    loads = [
        pltpu.make_async_copy(
            c_hbm.at[pl.ds(256 * t, 256), pl.ds(128 * s, 128)], df.at[8 * s + t],
            local_sem.at[11 + 8 * s + t],
        )
        for s in range(2)
        for t in range(8)
    ]
    order = [lax.rem(2 * (1 - c) + s, 4) for s in range(4)]
    wloads = [
        pltpu.make_async_copy(w_hbm.at[order[s]], w.at[order[s]], local_sem.at[2 + s])
        for s in range(4)
    ]
    xloads = [
        pltpu.make_async_copy(x_hbm.at[:, pl.ds(128 * q, 128)], imf.at[q], local_sem.at[6 + q])
        for q in range(4)
    ]
    for load in loads + wloads[:1] + xloads + wloads[1:]:
        load.start()

    barrier = pltpu.get_barrier_semaphore()
    pl.semaphore_signal(barrier, inc=1, device_id=place.peer("c", 1), device_id_type=MESH)
    for axis in ("x", "y", "z"):
        for d in (1, 2, 3):
            pl.semaphore_signal(barrier, inc=1, device_id=place.peer(axis, d), device_id_type=MESH)

    sender = Sender(place, send_sem, recv_sem)

    for n, load in enumerate(loads):
        load.wait()
        s, t = n // 8, n % 8
        cols[256 * t : 256 * t + 256, 128 * s : 128 * s + 128] = df[n].astype(BF16)
    for q, load in enumerate(xloads):
        load.wait()
        h, lo = split(imf[q])
        xh[:, 128 * q : 128 * q + 128] = h
        xw[:, 128 * q : 128 * q + 128] = lo

    cores = [
        RowSum(sender, 1024, cp.at[j], csib.at[j], carr.at[j], cfull.at[j]) for j in range(2)
    ]
    for s in range(4):
        e = order[s]
        wloads[s].wait()
        at = pl.ds(pl.multiple_of(e * 256, 256), 256)

        def project(i, carry, e=e, at=at):
            r = pl.ds(pl.multiple_of(i * 224, 32), 224)
            value = dot(w[e, r, :], cols[...], 1, 0)
            pf[r, :] = value
            h, lo = split(value)
            ph[r, at] = h
            pw[r, at] = lo
            return carry

        lax.fori_loop(0, 4, project, 0)
        h, lo = split(pf[...].T)
        pth[at, :] = h
        ptw[at, :] = lo
        value = dot3(pth[at, :], ptw[at, :], xh[...], xw[...], 1, 0)
        cp[0, at, :] = value[:, :256]
        cp[1, at, :] = value[:, 256:]
        if s == 1:
            pl.semaphore_wait(barrier, 10)
            for one in cores:
                one.start()
    for one in cores:
        one.scatter()
    for one in cores:
        one.reduce()

    planes = [
        PlaneSum(
            sender, "xy"[q % 2], "yx"[q % 2], ip.at[q], iarr1.at[q], ihalf.at[q], iarr2.at[q],
            imf.at[q],
        )
        for q in range(4)
    ]
    for j in range(2):
        cores[j].forward()
        cores[j].finish()
        h, lo = split(cfull[j])
        ch[...] = h
        cw[...] = lo

        def image(i, carry, j=j):
            r = pl.ds(pl.multiple_of(i * 224, 32), 224)
            value = dot3(ph[r, :], pw[r, :], ch[...], cw[...], 1, 0)
            ip[2 * j, r, :] = value[:, :128]
            ip[2 * j + 1, r, :] = value[:, 128:]
            return carry

        lax.fori_loop(0, 4, image, 0)
        planes[2 * j].start()
        planes[2 * j + 1].start()
    for one in planes:
        one.reduce1()
    for one in planes:
        one.reduce2()
    for one in planes:
        one.gather()

    def gram_part(i, j):
        a, b = slice(256 * i, 256 * i + 256), slice(256 * j, 256 * j + 256)
        return dot3(xh[:, a], xw[:, a], xh[:, b], xw[:, b], 0, 0)

    for q in range(4):
        planes[q].finish()
        h, lo = split(imf[q])
        xh[:, 128 * q : 128 * q + 128] = h
        xw[:, 128 * q : 128 * q + 128] = lo
        if q == 1:
            gp[0:256] = gram_part(0, 0)
    gp[256:512] = gram_part(0, 1)
    gp[512:768] = gram_part(1, 1)
    grams = RowSum(sender, 768, gp, gsib, garr, gfull)
    grams.start()
    backs = [
        RowSum(sender, 1024, cp.at[j], csib.at[j], carr.at[j], cfull.at[j]) for j in range(2)
    ]

    def under(j):
        def body(i, carry):
            r = pl.ds(pl.multiple_of(i * 256, 256), 256)
            a = slice(256 * j, 256 * j + 256)
            cp[j, r, :] = dot3(pth[r, :], ptw[r, :], xh[:, a], xw[:, a], 1, 0)
            return carry

        lax.fori_loop(0, 4, body, 0)

    grams.scatter()
    under(0)
    grams.reduce()
    under(1)
    grams.forward()
    backs[0].start()
    backs[1].start()
    grams.finish()
    backs[0].scatter()
    backs[1].scatter()
    gram[0:256, 0:256] = gfull[0:256]
    gram[0:256, 256:512] = gfull[256:512]
    gram[256:512, 256:512] = gfull[512:768]

    def between(k):
        if k == 1:
            backs[0].reduce()
            backs[1].reduce()
        if k == 3:
            backs[0].forward()
            backs[1].forward()

    inverse_factor(R1, gram, inv, between)
    h, lo = split(inv[...] * math.sqrt(D))
    vh[...] = h
    vw[...] = lo

    def row_basis(i, carry):
        r = pl.ds(pl.multiple_of(i * 224, 32), 224)
        value = dot3(xh[r, :], xw[r, :], vh[...], vw[...], 1, 1)
        rb[r, :] = value
        h, lo = split(value)
        xh[r, :] = h
        xw[r, :] = lo
        return carry

    lax.fori_loop(0, 4, row_basis, 0)
    rb_store = pltpu.make_async_copy(rb, rb_hbm, local_sem.at[10])
    rb_store.start()
    backs[0].finish()
    backs[1].finish()

    def core_two(i, carry):
        r = pl.ds(pl.multiple_of(i * 256, 256), 256)
        h, lo = split(jnp.concatenate([cfull[0, r, :], cfull[1, r, :]], axis=1))
        h, lo = split(dot3(h, lo, vh[...], vw[...], 1, 1))
        th[r, :] = h
        tw[r, :] = lo
        return carry

    lax.fori_loop(0, 4, core_two, 0)

    def back(i, carry):
        r = pl.ds(pl.multiple_of(i * 256, 256), 256)
        pth[r, :] = dot3(th[r, :], tw[r, :], xh[...], xw[...], 1, 1).astype(BF16)
        return carry

    lax.fori_loop(0, 4, back, 0)

    def column_image(i, carry, half):
        f = pl.multiple_of(half * 1024 + i * 256, 256)
        value = dot(pth[0:256, :], w[0, :, pl.ds(f, 256)], 1, 0)
        for e in range(1, 4):
            value = value + dot(pth[256 * e : 256 * e + 256, :], w[e, :, pl.ds(f, 256)], 1, 0)
        s = half * 8 + i * 2
        dp[s] = value[:, :128]
        dp[s + 1] = value[:, 128:]
        return carry

    lax.fori_loop(0, 4, functools.partial(column_image, half=1 - c), 0)
    swap = sender.copy(dp.at[pl.ds((1 - c) * 8, 8)], dsib, "c", 1)
    swap.start()
    lax.fori_loop(0, 4, functools.partial(column_image, half=c), 0)
    groups = [("zxy", 0, 3), ("xyz", 3, 3), ("yzx", 6, 2)]
    cubes = [
        CubeSum(sender, axes, u0, n, dp, darr1, dsum1, darr2, dsum2, darr3, df)
        for axes, u0, n in groups
    ]
    swap.wait()
    for one, (axes, u0, n) in zip(cubes, groups):
        mine = pl.ds(c * 8 + u0, n)
        dp[mine] = dp[mine] + dsib[pl.ds(u0, n)]
        one.start()
    for step in ("reduce1", "reduce2", "reduce3", "gather", "across", "finish"):
        for one in cubes:
            getattr(one, step)()

    for s in range(16):
        h, lo = split(df[s])
        if s == 0:
            value = dot3(h, lo, h, lo, 1, 1)
        else:
            value = value + dot3(h, lo, h, lo, 1, 1)
    gram[0:256, 0:256] = value
    inverse_factor(R2, gram.at[0:256, 0:256], inv.at[0:256, 0:256])
    h, lo = split(inv[0:256, 0:256] * math.sqrt(F))
    vh[0:256, 0:256] = h
    vw[0:256, 0:256] = lo
    stores = []
    for s in range(16):
        h, lo = split(df[s].T)
        value = dot3(h, lo, vh[0:256, 0:256], vw[0:256, 0:256], 1, 1)
        dp[s // 2, 128 * (s % 2) : 128 * (s % 2) + 128] = value[:, :128]
        dp[8 + s // 2, 128 * (s % 2) : 128 * (s % 2) + 128] = value[:, 128:]
        if s % 2:
            t = s // 2
            for g in range(2):
                store = pltpu.make_async_copy(
                    dp.at[8 * g + t],
                    cb_hbm.at[pl.ds(256 * t, 256), pl.ds(128 * g, 128)],
                    local_sem.at[11 + 2 * t + g],
                )
                store.start()
                stores.append(store)
    for store in stores:
        store.wait()
    rb_store.wait()


COPIES = 160


def shards(weights, prev_rows, prev_cols):
    vm = pltpu.VMEM
    return pl.pallas_call(
        kernel,
        name="orthogonal_step",
        out_shape=(
            jax.ShapeDtypeStruct((ROWS, R1), F32),
            jax.ShapeDtypeStruct((F, R2), F32),
        ),
        in_specs=[pl.BlockSpec(memory_space=pl.ANY)] * 3,
        out_specs=[pl.BlockSpec(memory_space=pl.ANY)] * 2,
        scratch_shapes=[
            vm((LOCAL, ROWS, F), BF16),
            vm((ROWS, 1024), BF16), vm((ROWS, 1024), BF16),
            vm((1024, ROWS), BF16), vm((1024, ROWS), BF16),
            vm((ROWS, R1), BF16), vm((ROWS, R1), BF16),
            vm((F, R2), BF16), vm((ROWS, R2), F32),
            vm((2, 1024, 256), F32), vm((2, 512, 256), F32), vm((2, 3, 128, 256), F32),
            vm((2, 1024, 256), F32), vm((1024, 256), BF16), vm((1024, 256), BF16),
            vm((4, ROWS, 128), F32), vm((4, 3, 224, 128), F32), vm((4, 224, 128), F32),
            vm((4, 3, 56, 128), F32), vm((4, ROWS, 128), F32),
            vm((768, 256), F32), vm((384, 256), F32), vm((3, 96, 256), F32), vm((768, 256), F32),
            vm((R1, R1), F32), vm((R1, R1), F32), vm((R1, R1), BF16), vm((R1, R1), BF16),
            vm((1024, R1), BF16), vm((1024, R1), BF16),
            vm((ROWS, R1), F32),
            vm((16, 256, 128), F32), vm((8, 256, 128), F32), vm((3, 8, 64, 128), F32),
            vm((8, 64, 128), F32), vm((3, 8, 16, 128), F32), vm((8, 16, 128), F32),
            vm((4, 8, 16, 128), F32), vm((16, 256, 128), F32),
            pltpu.SemaphoreType.DMA((32,)),
            pltpu.SemaphoreType.DMA((COPIES,)),
            pltpu.SemaphoreType.DMA((COPIES,)),
        ],
        compiler_params=pltpu.CompilerParams(
            collective_id=0, has_side_effects=True, vmem_limit_bytes=62 * 2**20
        ),
        cost_estimate=pl.CostEstimate(flops=12 * 10**9, bytes_accessed=25 * 10**6, transcendentals=0),
    )(weights, prev_rows, prev_cols)


def solution(mesh):
    placed = (P("expert", "row", None), P("row", None), P())
    return jax.shard_map(
        shards, mesh=mesh, in_specs=placed, out_specs=(P("row", None), P()), check_vma=False
    )
```

```python
import functools
import math

import jax
import jax.numpy as jnp
from jax import lax
from jax.experimental import pallas as pl
from jax.experimental.pallas import tpu as pltpu
from jax.sharding import PartitionSpec as P

D = 7168
F = 2048
R1 = 512
R2 = 256
ROWS = 896
LOCAL = 4
MESH = pl.DeviceIdType.MESH
HIGHEST = lax.Precision.HIGHEST
F32 = jnp.float32
BF16 = jnp.bfloat16


def dot(a, b, ca, cb, precision=None):
    return lax.dot_general(
        a, b, (((ca,), (cb,)), ((), ())), precision=precision, preferred_element_type=F32
    )


def split(value):
    high = value.astype(BF16)
    return high, (value - high.astype(F32)).astype(BF16)


def dot3(ah, al, bh, bl, ca, cb):
    return dot(ah, bh, ca, cb) + (dot(ah, bl, ca, cb) + dot(al, bh, ca, cb))


def dot3n(ah, al, both, ca, cb):
    wide = dot(ah, both[...], ca, cb)
    high = both[:, :128] if cb == 0 else both[:128, :]
    return wide[:, :128] + (wide[:, 128:] + dot(al, high, ca, cb))


def lane_of(block, j):
    return jnp.broadcast_to(block[:, j : j + 1], (8, 128))


def row_of(block, k):
    return jnp.broadcast_to(block[k : k + 1, :], (8, 128))


def inverse_factor_of_tile(blocks, hooks={}):
    count = 16
    sub = lax.broadcasted_iota(jnp.int32, (8, 128), 0)
    lane = lax.broadcasted_iota(jnp.int32, (8, 128), 1)
    left = list(blocks)
    right = [jnp.where(lane == sub + 8 * b, 1.0, 0.0).astype(F32) for b in range(count)]
    for b in range(count):
        if b in hooks:
            hooks[b]()
        columns = [lane_of(left[b], 8 * b + j) for j in range(8)]
        corner = {(k, j): row_of(columns[j], k) for j in range(8) for k in range(j, 8)}
        last = b == count - 1
        lrows = None if last else [row_of(left[b], k) for k in range(8)]
        rrows = [row_of(right[b], k) for k in range(8)]
        roots, low = [], {}
        for i in range(8):
            root = lax.rsqrt(corner[i, i])
            roots.append(root)
            for k in range(i + 1, 8):
                low[k, i] = corner[k, i] * root
            for j in range(i + 1, 8):
                for k in range(j, 8):
                    corner[k, j] = corner[k, j] - low[k, i] * low[j, i]
            rrows[i] = rrows[i] * root
            for k in range(i + 1, 8):
                rrows[k] = rrows[k] - low[k, i] * rrows[i]
            if not last:
                lrows[i] = lrows[i] * root
                for k in range(i + 1, 8):
                    lrows[k] = lrows[k] - low[k, i] * lrows[i]
        whole = rrows[7]
        for i in range(6, -1, -1):
            whole = jnp.where(sub == i, rrows[i], whole)
        right[b] = whole
        for t in range(b + 1, count):
            q = [lane_of(left[t], 8 * b + j) for j in range(8)]
            lt, rt = left[t], right[t]
            for i in range(8):
                term = q[i] * roots[i]
                for k in range(i + 1, 8):
                    q[k] = q[k] - low[k, i] * term
                lt = lt - term * lrows[i]
                rt = rt - term * rrows[i]
            left[t], right[t] = lt, rt
    return right


def factor_step(q, column, inverse, hooks={}):
    o = 128 * q
    if q:
        lead = inverse[0:o, 0:o]
        upper = dot(lead, column[0:o, :], 1, 0, HIGHEST)
        column[o : o + 128, :] = column[o : o + 128, :] - dot(upper, upper, 0, 0, HIGHEST)
        rest = dot(upper, lead, 0, 0, HIGHEST)
    rows = inverse_factor_of_tile([column[o + 8 * b : o + 8 * b + 8, :] for b in range(16)], hooks)
    own = jnp.concatenate(rows, axis=0)
    inverse[o : o + 128, o : o + 128] = own
    if q:
        inverse[o : o + 128, 0:o] = -dot(own, rest, 1, 0, HIGHEST)


class Place:
    def __init__(self):
        expert, row = lax.axis_index("expert"), lax.axis_index("row")
        self.at = {
            "x": lax.div(expert, 4), "y": lax.rem(expert, 4),
            "z": lax.div(row, 2), "c": lax.rem(row, 2),
        }

    def index(self, axis, d):
        return lax.rem(self.at[axis] + d, 4)

    def peer(self, axis, d):
        at = dict(self.at)
        at[axis] = lax.rem(at[axis] + d, 2 if axis == "c" else 4)
        return (at["x"] * 4 + at["y"], at["z"] * 2 + at["c"])


class Sender:
    def __init__(self, place, send_sem, recv_sem):
        self.place, self.send_sem, self.recv_sem, self.used = place, send_sem, recv_sem, 0

    def copy(self, source, target, axis, d):
        n = self.used
        self.used += 1
        return pltpu.make_async_remote_copy(
            src_ref=source, dst_ref=target, send_sem=self.send_sem.at[n],
            recv_sem=self.recv_sem.at[n], device_id=self.place.peer(axis, d), device_id_type=MESH,
        )


class RowSum:
    def __init__(self, sender, rows, part, sibling, arrived, full):
        place = sender.place
        c = place.at["c"]
        half, chunk = rows // 2, rows // 8
        self.half, self.chunk, self.c = half, chunk, c
        self.part, self.sibling, self.arrived, self.full = part, sibling, arrived, full
        self.base = c * half
        other = (1 - c) * half
        self.place = place
        self.swap = sender.copy(part.at[pl.ds(other, half)], sibling, "c", 1)
        self.spread = [
            sender.copy(
                part.at[pl.ds(self.base + place.index("z", d) * chunk, chunk)],
                arrived.at[d - 1], "z", d,
            )
            for d in (1, 2, 3)
        ]
        self.mine = self.base + place.at["z"] * chunk
        own = full.at[pl.ds(self.mine, chunk)]
        self.gather = [sender.copy(own, own, "z", d) for d in (1, 2, 3)]
        self.across = [sender.copy(own, own, "c", 1)]
        for d in (1, 2, 3):
            got = full.at[pl.ds(self.base + place.index("z", 4 - d) * chunk, chunk)]
            self.across.append(sender.copy(got, got, "c", 1))

    def start(self):
        self.swap.start()

    def scatter(self):
        self.swap.wait_recv()
        for d in (1, 2, 3, 0):
            p = self.place.index("z", d)
            there = pl.ds(self.base + p * self.chunk, self.chunk)
            self.part[there] = self.part[there] + self.sibling[pl.ds(p * self.chunk, self.chunk)]
            if d:
                self.spread[d - 1].start()

    def reduce(self):
        for copy in self.spread:
            copy.wait_recv()
        there = pl.ds(self.mine, self.chunk)
        self.full[there] = (self.part[there] + self.arrived[0]) + (
            self.arrived[1] + self.arrived[2]
        )
        for copy in self.gather:
            copy.start()
        self.across[0].start()

    def forward(self):
        for d in (1, 2, 3):
            self.gather[d - 1].wait_recv()
            self.across[d].start()

    def finish(self):
        for copy in self.across:
            copy.wait()
        self.swap.wait_send()
        for copy in self.spread + self.gather:
            copy.wait_send()


class PlaneSum:
    def __init__(self, sender, first, second, r0, n, part, arrived1, half, arrived2, full):
        place = sender.place
        m1, m2 = place.at[first], place.at[second]
        wide, narrow = n // 4, n // 16
        self.part, self.arrived1, self.half = part, arrived1, half
        self.arrived2, self.full = arrived2, full
        at1, at2 = pl.ds(r0 // 4, wide), pl.ds(r0 // 16, narrow)
        self.at1, self.at2 = at1, at2
        self.mine1 = pl.ds(r0 + m1 * wide, wide)
        self.from2 = pl.ds(r0 // 4 + m2 * narrow, narrow)
        self.mine2 = pl.ds(r0 + m1 * wide + m2 * narrow, narrow)
        self.one = [
            sender.copy(
                part.at[pl.ds(r0 + place.index(first, d) * wide, wide)],
                arrived1.at[d - 1, at1], first, d,
            )
            for d in (1, 2, 3)
        ]
        self.two = [
            sender.copy(
                half.at[pl.ds(r0 // 4 + place.index(second, d) * narrow, narrow)],
                arrived2.at[d - 1, at2], second, d,
            )
            for d in (1, 2, 3)
        ]
        own = full.at[self.mine2]
        self.three = [sender.copy(own, own, second, d) for d in (1, 2, 3)]
        strip = full.at[self.mine1]
        self.four = [sender.copy(strip, strip, first, d) for d in (1, 2, 3)]

    def start(self):
        for copy in self.one:
            copy.start()

    def reduce1(self):
        for copy in self.one:
            copy.wait_recv()
        a, at = self.arrived1, self.at1
        self.half[at] = (self.part[self.mine1] + a[0, at]) + (a[1, at] + a[2, at])
        for copy in self.two:
            copy.start()

    def reduce2(self):
        for copy in self.two:
            copy.wait_recv()
        a, at = self.arrived2, self.at2
        self.full[self.mine2] = (self.half[self.from2] + a[0, at]) + (a[1, at] + a[2, at])
        for copy in self.three:
            copy.start()

    def gather(self):
        for copy in self.three:
            copy.wait_recv()
        for copy in self.four:
            copy.start()

    def finish(self):
        for copy in self.four:
            copy.wait_recv()
        for copy in self.one + self.two + self.three + self.four:
            copy.wait_send()


class Pair:
    def __init__(self, *parts):
        self.parts = parts

    def __getattr__(self, name):
        def both():
            for part in self.parts:
                getattr(part, name)()

        return both


class CubeSum:
    def __init__(self, sender, axes, u0, n, part, arrived1, sum1, arrived2, sum2, arrived3, full):
        place = sender.place
        a1, a2, a3 = axes
        m1, m2, m3 = (place.at[a] for a in axes)
        base = place.at["c"] * 8 + u0
        slabs = pl.ds(u0, n)
        self.slabs, self.m1, self.m2, self.m3, self.base, self.n = slabs, m1, m2, m3, base, n
        self.part, self.arrived1, self.sum1 = part, arrived1, sum1
        self.arrived2, self.sum2, self.arrived3, self.full = arrived2, sum2, arrived3, full
        self.one = [
            sender.copy(
                part.at[pl.ds(base, n), pl.ds(place.index(a1, d) * 64, 64)],
                arrived1.at[d - 1, slabs], a1, d,
            )
            for d in (1, 2, 3)
        ]
        self.two = [
            sender.copy(
                sum1.at[slabs, pl.ds(place.index(a2, d) * 16, 16)],
                arrived2.at[d - 1, slabs], a2, d,
            )
            for d in (1, 2, 3)
        ]
        self.three = [
            sender.copy(arrived3.at[m3, slabs], arrived3.at[m3, slabs], a3, d) for d in (1, 2, 3)
        ]
        own = full.at[pl.ds(base, n), pl.ds(m1 * 64 + m2 * 16, 16)]
        self.four = [sender.copy(own, own, a2, d) for d in (1, 2, 3)]
        wide = full.at[pl.ds(base, n), pl.ds(m1 * 64, 64)]
        self.five = [sender.copy(wide, wide, a1, d) for d in (1, 2, 3)]
        whole = full.at[pl.ds(base, n)]
        self.six = sender.copy(whole, whole, "c", 1)

    def start(self):
        for copy in self.one:
            copy.start()

    def reduce1(self):
        for copy in self.one:
            copy.wait_recv()
        a, s = self.arrived1, self.slabs
        own = self.part[pl.ds(self.base, self.n), pl.ds(self.m1 * 64, 64)]
        self.sum1[s] = (own + a[0, s]) + (a[1, s] + a[2, s])
        for copy in self.two:
            copy.start()

    def reduce2(self):
        for copy in self.two:
            copy.wait_recv()
        a, s = self.arrived2, self.slabs
        own = self.sum1[s, pl.ds(self.m2 * 16, 16)]
        self.arrived3[self.m3, s] = (own + a[0, s]) + (a[1, s] + a[2, s])
        for copy in self.three:
            copy.start()

    def reduce3(self):
        for copy in self.three:
            copy.wait()
        a, s = self.arrived3, self.slabs
        self.full[pl.ds(self.base, self.n), pl.ds(self.m1 * 64 + self.m2 * 16, 16)] = (
            a[0, s] + a[1, s]
        ) + (a[2, s] + a[3, s])
        for copy in self.four:
            copy.start()

    def gather(self):
        for copy in self.four:
            copy.wait_recv()
        for copy in self.five:
            copy.start()

    def across(self):
        for copy in self.five:
            copy.wait_recv()
        self.six.start()

    def finish(self):
        self.six.wait()
        for copy in self.one + self.two + self.four + self.five:
            copy.wait_send()


def kernel(
    w_hbm, x_hbm, c_hbm, rb_hbm, cb_hbm,
    w, ph, pw, pth, ptw, xcat, xth, xtw, cols, pf,
    cp, csib, carr, cfull, ccat,
    ip, iarr1, ihalf, iarr2, imf,
    gp, gsib, garr, gfull, inv, vcat, th, tw, gh, gw,
    rb, dp, dsib, darr1, dsum1, darr2, dsum2, darr3, df,
    local_sem, send_sem, recv_sem,
):
    place = Place()
    c = place.at["c"]
    loads = [
        pltpu.make_async_copy(
            c_hbm.at[pl.ds(256 * t, 256), pl.ds(128 * s, 128)], df.at[8 * s + t],
            local_sem.at[11 + 8 * s + t],
        )
        for s in range(2)
        for t in range(8)
    ]
    order = [lax.rem(2 * (1 - c) + s, 4) for s in range(4)]
    wloads = [
        pltpu.make_async_copy(w_hbm.at[order[s]], w.at[order[s]], local_sem.at[2 + s])
        for s in range(4)
    ]
    xloads = [
        pltpu.make_async_copy(x_hbm.at[:, pl.ds(128 * q, 128)], imf.at[q], local_sem.at[6 + q])
        for q in range(4)
    ]
    for load in loads + wloads[:1]:
        load.start()

    barrier = pltpu.get_barrier_semaphore()
    pl.semaphore_signal(barrier, inc=1, device_id=place.peer("c", 1), device_id_type=MESH)
    for axis in ("x", "y", "z"):
        for d in (1, 2, 3):
            pl.semaphore_signal(barrier, inc=1, device_id=place.peer(axis, d), device_id_type=MESH)

    sender = Sender(place, send_sem, recv_sem)

    for n, load in enumerate(loads):
        load.wait()
        s, t = n // 8, n % 8
        cols[256 * t : 256 * t + 256, 128 * s : 128 * s + 128] = df[n].astype(BF16)
        if n == 11:
            wloads[1].start()
    for load in xloads:
        load.start()

    def row_sum(q):
        return RowSum(sender, 1024, cp.at[q], csib.at[q], carr.at[q], cfull.at[q])

    A = [row_sum(q) for q in range(4)]
    for s in range(4):
        e = order[s]
        wloads[s].wait()
        if s < 2:
            wloads[s + 2].start()
        at = pl.ds(pl.multiple_of(e * 256, 256), 256)

        def project(i, carry, e=e, at=at):
            r = pl.ds(pl.multiple_of(i * 448, 64), 448)
            value = dot(w[e, r, :], cols[...], 1, 0)
            pf[r, :] = value
            h, lo = split(value)
            ph[r, at] = h
            pw[r, at] = lo
            return carry

        lax.fori_loop(0, 2, project, 0)
        h, lo = split(pf[...].T)
        pth[at, :] = h
        ptw[at, :] = lo
        if s == 0:
            for q, load in enumerate(xloads):
                load.wait()
                h, lo = split(imf[q])
                xcat[q, :, :128] = h
                xcat[q, :, 128:] = lo
        if s % 2 == 0:
            continue
        pair = pl.ds(pl.multiple_of((1 - c if s == 1 else c) * 512, 512), 512)
        for q in range(0, 4, 2):
            right = jnp.concatenate([xcat[q, :, :128], xcat[q + 1, :, :128]], axis=1)
            low = dot(ptw[pair, :], right, 1, 0)
            for t in range(2):
                wide = dot(pth[pair, :], xcat[q + t], 1, 0)
                cp[q + t, pair, :] = wide[:, :128] + (
                    wide[:, 128:] + low[:, 128 * t : 128 * t + 128]
                )
        if s == 1:
            pl.semaphore_wait(barrier, 10)
            for one in A:
                one.start()

    def plane_sum(q):
        refs = (ip.at[q], iarr1.at[q], ihalf.at[q], iarr2.at[q], imf.at[q])
        return Pair(
            PlaneSum(sender, "x", "y", 0, 512, *refs), PlaneSum(sender, "y", "x", 512, 384, *refs)
        )

    B = [plane_sum(q) for q in range(4)]

    def image(q):
        h, lo = split(cfull[q])
        ccat[:, :128] = h
        ccat[:, 128:] = lo

        def body(i, carry):
            r = pl.ds(pl.multiple_of(i * 448, 64), 448)
            ip[q, r, :] = dot3n(ph[r, :], pw[r, :], ccat, 1, 0)
            return carry

        lax.fori_loop(0, 2, body, 0)
        B[q].start()

    C, G = [], []

    def gram(q):
        h, lo = split(imf[q])
        xcat[q, :, :128] = h
        xcat[q, :, 128:] = lo
        h, lo = split(imf[q].T)
        r = slice(128 * q, 128 * q + 128)
        xth[r, :] = h
        xtw[r, :] = lo
        n = 128 * (q + 1)
        at, half, part = 64 * q * (q + 1), 32 * q * (q + 1), 8 * q * (q + 1)
        own = gp.at[pl.ds(at, n)]
        own[...] = dot3n(xth[0:n, :], xtw[0:n, :], xcat.at[q], 1, 0)
        C.append(
            RowSum(
                sender, n, own, gsib.at[pl.ds(half, n // 2)],
                garr.at[:, pl.ds(part, n // 8)], gfull.at[pl.ds(at, n)],
            )
        )
        C[q].start()

    def under(q):
        def body(i, carry):
            r = pl.ds(pl.multiple_of(i * 512, 512), 512)
            cp[q, r, :] = dot3n(pth[r, :], ptw[r, :], xcat.at[q], 1, 0)
            return carry

        lax.fori_loop(0, 2, body, 0)
        G.append(row_sum(q))
        G[q].start()

    def factor(q, hooks={}):
        factor_step(q, C[q].full, inv, hooks)

    def basis(q):
        n = 128 * (q + 1)
        h, lo = split(inv[n - 128 : n, 0:n] * math.sqrt(D))
        vcat[0:128, 0:n] = h
        vcat[128:256, 0:n] = lo
        high = jnp.concatenate([xcat[p, :, :128] for p in range(q + 1)], axis=1)
        low = jnp.concatenate([xcat[p, :, 128:] for p in range(q + 1)], axis=1)
        value = dot3n(high, low, vcat.at[:, 0:n], 1, 1)
        rb[q] = value
        h, lo = split(value)
        ph[:, n - 128 : n] = h
        ph[:, 384 + n : 512 + n] = lo
        store = pltpu.make_async_copy(
            rb.at[q], rb_hbm.at[:, pl.ds(128 * q, 128)], local_sem.at[27 + q]
        )
        store.start()
        stores.append(store)

    def core_two(q):
        n = 128 * (q + 1)
        h, lo = split(cfull[q])
        gh[:, n - 128 : n] = h
        gw[:, n - 128 : n] = lo
        h, lo = split(inv[n - 128 : n, 0:n] * math.sqrt(D))
        vcat[0:128, 0:n] = h
        vcat[128:256, 0:n] = lo
        h, lo = split(dot3n(gh[:, 0:n], gw[:, 0:n], vcat.at[:, 0:n], 1, 1))
        th[:, n - 128 : n] = h
        tw[:, n - 128 : n] = lo

    def steps(*calls):
        def run():
            for call in calls:
                call()

        return run

    inv[...] = jnp.zeros_like(inv)
    stores = []
    A[0].scatter()
    A[1].scatter()
    A[0].reduce()
    A[1].reduce()
    A[2].scatter()
    A[3].scatter()
    A[0].forward()
    A[0].finish()
    image(0)
    A[1].forward()
    A[1].finish()
    image(1)
    A[2].reduce()
    B[0].reduce1()
    A[3].reduce()
    A[2].forward()
    B[1].reduce1()
    B[0].reduce2()
    A[2].finish()
    image(2)
    B[0].gather()
    B[1].reduce2()
    A[3].forward()
    A[3].finish()
    image(3)
    B[2].reduce1()
    B[0].finish()
    gram(0)
    C[0].scatter()
    under(0)
    B[1].gather()
    B[3].reduce1()
    B[2].reduce2()
    C[0].reduce()
    C[0].forward()
    C[0].finish()
    factor(0, {
        4: steps(
            lambda: G[0].scatter(),
            lambda: B[3].reduce2(),
            lambda: B[2].gather(),
        ),
    })
    G[0].reduce()
    B[3].gather()
    B[1].finish()
    gram(1)
    under(1)
    C[1].scatter()
    B[2].finish()
    gram(2)
    under(2)
    C[2].scatter()
    C[1].reduce()
    B[3].finish()
    gram(3)
    under(3)
    C[3].scatter()
    C[2].reduce()
    G[1].scatter()
    C[1].forward()
    C[1].finish()
    factor(1, {
        4: steps(
            lambda: G[3].scatter(),
        ),
        12: steps(
            lambda: C[3].reduce(),
            lambda: C[2].forward(),
            lambda: G[1].reduce(),
        ),
    })
    C[2].finish()
    factor(2, {
        4: steps(
            lambda: G[3].reduce(),
            lambda: G[2].scatter(),
            lambda: basis(1),
            lambda: C[3].forward(),
        ),
    })
    basis(2)
    C[3].finish()
    factor(3, {
        12: steps(
            lambda: G[1].forward(),
            lambda: G[2].reduce(),
        ),
    })
    basis(3)
    G[0].forward()
    G[0].finish()
    core_two(0)
    G[1].finish()
    core_two(1)
    G[2].forward()
    G[3].forward()
    basis(0)
    G[2].finish()
    core_two(2)
    G[3].finish()
    core_two(3)

    def back(i, carry):
        r = pl.ds(pl.multiple_of(i * 256, 256), 256)
        pth[r, :] = dot3(th[r, :], tw[r, :], ph[:, 0:512], ph[:, 512:1024], 1, 1).astype(BF16)
        return carry

    lax.fori_loop(0, 4, back, 0)

    def column_image(i, carry, half):
        f = pl.multiple_of(half * 1024 + i * 256, 256)
        value = dot(pth[0:256, :], w[0, :, pl.ds(f, 256)], 1, 0)
        for e in range(1, 4):
            value = value + dot(pth[256 * e : 256 * e + 256, :], w[e, :, pl.ds(f, 256)], 1, 0)
        s = half * 8 + i * 2
        dp[s] = value[:, :128]
        dp[s + 1] = value[:, 128:]
        return carry

    lax.fori_loop(0, 4, functools.partial(column_image, half=1 - c), 0)
    swap = sender.copy(dp.at[pl.ds((1 - c) * 8, 8)], dsib, "c", 1)
    swap.start()
    lax.fori_loop(0, 4, functools.partial(column_image, half=c), 0)
    groups = [("zxy", 0, 3), ("xyz", 3, 3), ("yzx", 6, 2)]
    cubes = [
        CubeSum(sender, axes, u0, n, dp, darr1, dsum1, darr2, dsum2, darr3, df)
        for axes, u0, n in groups
    ]
    swap.wait()
    for one, (axes, u0, n) in zip(cubes, groups):
        mine = pl.ds(c * 8 + u0, n)
        dp[mine] = dp[mine] + dsib[pl.ds(u0, n)]
        one.start()
    for step in ("reduce1", "reduce2", "reduce3", "gather", "across", "finish"):
        for one in cubes:
            getattr(one, step)()

    for s in range(16):
        h, lo = split(df[s])
        if s == 0:
            value = dot3(h, lo, h, lo, 1, 1)
        else:
            value = value + dot3(h, lo, h, lo, 1, 1)
    gp[0:128, :] = value[0:128, 0:128]
    gp[128:384, :] = value[:, 128:256]
    factor_step(0, gp.at[0:128], inv)
    factor_step(1, gp.at[128:384], inv)
    h, lo = split(inv[0:256, 0:256] * math.sqrt(F))
    vcat[:, 0:256] = h
    vcat[:, 256:512] = lo
    for s in range(16):
        h, lo = split(df[s].T)
        value = dot3(h, lo, vcat[:, 0:256], vcat[:, 256:512], 1, 1)
        dp[s // 2, 128 * (s % 2) : 128 * (s % 2) + 128] = value[:, :128]
        dp[8 + s // 2, 128 * (s % 2) : 128 * (s % 2) + 128] = value[:, 128:]
        if s % 2:
            t = s // 2
            for g in range(2):
                store = pltpu.make_async_copy(
                    dp.at[8 * g + t],
                    cb_hbm.at[pl.ds(256 * t, 256), pl.ds(128 * g, 128)],
                    local_sem.at[11 + 2 * t + g],
                )
                store.start()
                stores.append(store)
    for store in stores:
        store.wait()


COPIES = 288


def shards(weights, prev_rows, prev_cols):
    vm = pltpu.VMEM
    return pl.pallas_call(
        kernel,
        name="orthogonal_step",
        out_shape=(
            jax.ShapeDtypeStruct((ROWS, R1), F32),
            jax.ShapeDtypeStruct((F, R2), F32),
        ),
        in_specs=[pl.BlockSpec(memory_space=pl.ANY)] * 3,
        out_specs=[pl.BlockSpec(memory_space=pl.ANY)] * 2,
        scratch_shapes=[
            vm((LOCAL, ROWS, F), BF16),
            vm((ROWS, 1024), BF16), vm((ROWS, 1024), BF16),
            vm((1024, ROWS), BF16), vm((1024, ROWS), BF16),
            vm((4, ROWS, 256), BF16), vm((R1, ROWS), BF16), vm((R1, ROWS), BF16),
            vm((F, R2), BF16), vm((ROWS, R2), F32),
            vm((4, 1024, 128), F32), vm((4, 512, 128), F32), vm((4, 3, 128, 128), F32),
            vm((4, 1024, 128), F32), vm((1024, 256), BF16),
            vm((4, ROWS, 128), F32), vm((4, 3, 224, 128), F32), vm((4, 224, 128), F32),
            vm((4, 3, 56, 128), F32), vm((4, ROWS, 128), F32),
            vm((1280, 128), F32), vm((640, 128), F32), vm((3, 160, 128), F32), vm((1280, 128), F32),
            vm((R1, R1), F32), vm((256, R1), BF16),
            vm((1024, R1), BF16), vm((1024, R1), BF16), vm((1024, R1), BF16), vm((1024, R1), BF16),
            vm((4, ROWS, 128), F32),
            vm((16, 256, 128), F32), vm((8, 256, 128), F32), vm((3, 8, 64, 128), F32),
            vm((8, 64, 128), F32), vm((3, 8, 16, 128), F32), vm((8, 16, 128), F32),
            vm((4, 8, 16, 128), F32), vm((16, 256, 128), F32),
            pltpu.SemaphoreType.DMA((32,)),
            pltpu.SemaphoreType.DMA((COPIES,)),
            pltpu.SemaphoreType.DMA((COPIES,)),
        ],
        compiler_params=pltpu.CompilerParams(
            collective_id=0, has_side_effects=True, vmem_limit_bytes=62 * 2**20
        ),
        cost_estimate=pl.CostEstimate(flops=12 * 10**9, bytes_accessed=25 * 10**6, transcendentals=0),
    )(weights, prev_rows, prev_cols)


def solution(mesh):
    placed = (P("expert", "row", None), P("row", None), P())
    return jax.shard_map(
        shards, mesh=mesh, in_specs=placed, out_specs=(P("row", None), P()), check_vma=False
    )
```

```python
import functools
import math

import jax
import jax.numpy as jnp
from jax import lax
from jax.experimental import pallas as pl
from jax.experimental.pallas import tpu as pltpu
from jax.sharding import PartitionSpec as P

D = 7168
F = 2048
R1 = 512
R2 = 256
ROWS = 896
LOCAL = 4
MESH = pl.DeviceIdType.MESH
HIGHEST = lax.Precision.HIGHEST
F32 = jnp.float32
BF16 = jnp.bfloat16


def dot(a, b, ca, cb, precision=None):
    return lax.dot_general(
        a, b, (((ca,), (cb,)), ((), ())), precision=precision, preferred_element_type=F32
    )


def split(value):
    high = value.astype(BF16)
    return high, (value - high.astype(F32)).astype(BF16)


def dot3(ah, al, bh, bl, ca, cb):
    return dot(ah, bh, ca, cb) + (dot(ah, bl, ca, cb) + dot(al, bh, ca, cb))


def dot3n(ah, al, both, ca, cb):
    wide = dot(ah, both[...], ca, cb)
    high = both[:, :128] if cb == 0 else both[:128, :]
    return wide[:, :128] + (wide[:, 128:] + dot(al, high, ca, cb))


def lane_of(block, j):
    return jnp.broadcast_to(block[:, j : j + 1], (8, 128))


def row_of(block, k):
    return jnp.broadcast_to(block[k : k + 1, :], (8, 128))


def inverse_factor_of_tile(blocks, hooks={}):
    count = 16
    sub = lax.broadcasted_iota(jnp.int32, (8, 128), 0)
    lane = lax.broadcasted_iota(jnp.int32, (8, 128), 1)
    left = list(blocks)
    right = [jnp.where(lane == sub + 8 * b, 1.0, 0.0).astype(F32) for b in range(count)]
    for b in range(count):
        if b in hooks:
            hooks[b]()
        columns = [lane_of(left[b], 8 * b + j) for j in range(8)]
        corner = {(k, j): row_of(columns[j], k) for j in range(8) for k in range(j, 8)}
        last = b == count - 1
        lrows = None if last else [row_of(left[b], k) for k in range(8)]
        rrows = [row_of(right[b], k) for k in range(8)]
        roots, low = [], {}
        for i in range(8):
            root = lax.rsqrt(corner[i, i])
            roots.append(root)
            for k in range(i + 1, 8):
                low[k, i] = corner[k, i] * root
            for j in range(i + 1, 8):
                for k in range(j, 8):
                    corner[k, j] = corner[k, j] - low[k, i] * low[j, i]
            rrows[i] = rrows[i] * root
            for k in range(i + 1, 8):
                rrows[k] = rrows[k] - low[k, i] * rrows[i]
            if not last:
                lrows[i] = lrows[i] * root
                for k in range(i + 1, 8):
                    lrows[k] = lrows[k] - low[k, i] * lrows[i]
        whole = rrows[7]
        for i in range(6, -1, -1):
            whole = jnp.where(sub == i, rrows[i], whole)
        right[b] = whole
        for t in range(b + 1, count):
            q = [lane_of(left[t], 8 * b + j) for j in range(8)]
            lt, rt = left[t], right[t]
            for i in range(8):
                term = q[i] * roots[i]
                for k in range(i + 1, 8):
                    q[k] = q[k] - low[k, i] * term
                lt = lt - term * lrows[i]
                rt = rt - term * rrows[i]
            left[t], right[t] = lt, rt
    return right


def factor_step(q, column, inverse, hooks={}):
    o = 128 * q
    if q:
        lead = inverse[0:o, 0:o]
        upper = dot(lead, column[0:o, :], 1, 0, HIGHEST)
        column[o : o + 128, :] = column[o : o + 128, :] - dot(upper, upper, 0, 0, HIGHEST)
        rest = dot(upper, lead, 0, 0, HIGHEST)
    rows = inverse_factor_of_tile([column[o + 8 * b : o + 8 * b + 8, :] for b in range(16)], hooks)
    own = jnp.concatenate(rows, axis=0)
    inverse[o : o + 128, o : o + 128] = own
    if q:
        inverse[o : o + 128, 0:o] = -dot(own, rest, 1, 0, HIGHEST)


class Place:
    def __init__(self):
        expert, row = lax.axis_index("expert"), lax.axis_index("row")
        self.at = {
            "x": lax.div(expert, 4), "y": lax.rem(expert, 4),
            "z": lax.div(row, 2), "c": lax.rem(row, 2),
        }

    def index(self, axis, d):
        return lax.rem(self.at[axis] + d, 4)

    def peer(self, axis, d):
        at = dict(self.at)
        at[axis] = lax.rem(at[axis] + d, 2 if axis == "c" else 4)
        return (at["x"] * 4 + at["y"], at["z"] * 2 + at["c"])


class Sender:
    def __init__(self, place, send_sem, recv_sem):
        self.place, self.send_sem, self.recv_sem, self.used = place, send_sem, recv_sem, 0

    def copy(self, source, target, axis, d):
        n = self.used
        self.used += 1
        return pltpu.make_async_remote_copy(
            src_ref=source, dst_ref=target, send_sem=self.send_sem.at[n],
            recv_sem=self.recv_sem.at[n], device_id=self.place.peer(axis, d), device_id_type=MESH,
        )


class RowSum:
    def __init__(self, sender, rows, part, sibling, arrived, full):
        place = sender.place
        c = place.at["c"]
        half, chunk = rows // 2, rows // 8
        self.half, self.chunk, self.c = half, chunk, c
        self.part, self.sibling, self.arrived, self.full = part, sibling, arrived, full
        self.base = c * half
        other = (1 - c) * half
        self.place = place
        self.swap = sender.copy(part.at[pl.ds(other, half)], sibling, "c", 1)
        self.spread = [
            sender.copy(
                part.at[pl.ds(self.base + place.index("z", d) * chunk, chunk)],
                arrived.at[d - 1], "z", d,
            )
            for d in (1, 2, 3)
        ]
        self.mine = self.base + place.at["z"] * chunk
        own = full.at[pl.ds(self.mine, chunk)]
        self.gather = [sender.copy(own, own, "z", d) for d in (1, 2, 3)]
        self.across = [sender.copy(own, own, "c", 1)]
        for d in (1, 2, 3):
            got = full.at[pl.ds(self.base + place.index("z", 4 - d) * chunk, chunk)]
            self.across.append(sender.copy(got, got, "c", 1))

    def start(self):
        self.swap.start()

    def scatter(self):
        self.swap.wait_recv()
        for d in (1, 2, 3, 0):
            p = self.place.index("z", d)
            there = pl.ds(self.base + p * self.chunk, self.chunk)
            self.part[there] = self.part[there] + self.sibling[pl.ds(p * self.chunk, self.chunk)]
            if d:
                self.spread[d - 1].start()

    def reduce(self):
        for copy in self.spread:
            copy.wait_recv()
        there = pl.ds(self.mine, self.chunk)
        self.full[there] = (self.part[there] + self.arrived[0]) + (
            self.arrived[1] + self.arrived[2]
        )
        for copy in self.gather:
            copy.start()
        self.across[0].start()

    def forward(self):
        for d in (1, 2, 3):
            self.gather[d - 1].wait_recv()
            self.across[d].start()

    def finish(self):
        for copy in self.across:
            copy.wait()
        self.swap.wait_send()
        for copy in self.spread + self.gather:
            copy.wait_send()


class PlaneSum:
    def __init__(self, sender, first, second, r0, n, part, arrived1, half, arrived2, full):
        place = sender.place
        m1, m2 = place.at[first], place.at[second]
        wide, narrow = n // 4, n // 16
        self.part, self.arrived1, self.half = part, arrived1, half
        self.arrived2, self.full = arrived2, full
        at1, at2 = pl.ds(r0 // 4, wide), pl.ds(r0 // 16, narrow)
        self.at1, self.at2 = at1, at2
        self.mine1 = pl.ds(r0 + m1 * wide, wide)
        self.from2 = pl.ds(r0 // 4 + m2 * narrow, narrow)
        self.mine2 = pl.ds(r0 + m1 * wide + m2 * narrow, narrow)
        self.one = [
            sender.copy(
                part.at[pl.ds(r0 + place.index(first, d) * wide, wide)],
                arrived1.at[d - 1, at1], first, d,
            )
            for d in (1, 2, 3)
        ]
        self.two = [
            sender.copy(
                half.at[pl.ds(r0 // 4 + place.index(second, d) * narrow, narrow)],
                arrived2.at[d - 1, at2], second, d,
            )
            for d in (1, 2, 3)
        ]
        own = full.at[self.mine2]
        self.three = [sender.copy(own, own, second, d) for d in (1, 2, 3)]
        strip = full.at[self.mine1]
        self.four = [sender.copy(strip, strip, first, d) for d in (1, 2, 3)]

    def start(self):
        for copy in self.one:
            copy.start()

    def reduce1(self):
        for copy in self.one:
            copy.wait_recv()
        a, at = self.arrived1, self.at1
        self.half[at] = (self.part[self.mine1] + a[0, at]) + (a[1, at] + a[2, at])
        for copy in self.two:
            copy.start()

    def reduce2(self):
        for copy in self.two:
            copy.wait_recv()
        a, at = self.arrived2, self.at2
        self.full[self.mine2] = (self.half[self.from2] + a[0, at]) + (a[1, at] + a[2, at])
        for copy in self.three:
            copy.start()

    def gather(self):
        for copy in self.three:
            copy.wait_recv()
        for copy in self.four:
            copy.start()

    def finish(self):
        for copy in self.four:
            copy.wait_recv()
        for copy in self.one + self.two + self.three + self.four:
            copy.wait_send()


class Pair:
    def __init__(self, *parts):
        self.parts = parts

    def __getattr__(self, name):
        def both():
            for part in self.parts:
                getattr(part, name)()

        return both


class CubeSum:
    def __init__(self, sender, axes, u0, n, part, arrived1, sum1, arrived2, sum2, arrived3, full):
        place = sender.place
        a1, a2, a3 = axes
        m1, m2, m3 = (place.at[a] for a in axes)
        base = place.at["c"] * 8 + u0
        slabs = pl.ds(u0, n)
        self.slabs, self.m1, self.m2, self.m3, self.base, self.n = slabs, m1, m2, m3, base, n
        self.part, self.arrived1, self.sum1 = part, arrived1, sum1
        self.arrived2, self.sum2, self.arrived3, self.full = arrived2, sum2, arrived3, full
        self.one = [
            sender.copy(
                part.at[pl.ds(base, n), pl.ds(place.index(a1, d) * 64, 64)],
                arrived1.at[d - 1, slabs], a1, d,
            )
            for d in (1, 2, 3)
        ]
        self.two = [
            sender.copy(
                sum1.at[slabs, pl.ds(place.index(a2, d) * 16, 16)],
                arrived2.at[d - 1, slabs], a2, d,
            )
            for d in (1, 2, 3)
        ]
        self.three = [
            sender.copy(arrived3.at[m3, slabs], arrived3.at[m3, slabs], a3, d) for d in (1, 2, 3)
        ]
        own = full.at[pl.ds(base, n), pl.ds(m1 * 64 + m2 * 16, 16)]
        self.four = [sender.copy(own, own, a2, d) for d in (1, 2, 3)]
        wide = full.at[pl.ds(base, n), pl.ds(m1 * 64, 64)]
        self.five = [sender.copy(wide, wide, a1, d) for d in (1, 2, 3)]
        whole = full.at[pl.ds(base, n)]
        self.six = sender.copy(whole, whole, "c", 1)

    def start(self):
        for copy in self.one:
            copy.start()

    def reduce1(self):
        for copy in self.one:
            copy.wait_recv()
        a, s = self.arrived1, self.slabs
        own = self.part[pl.ds(self.base, self.n), pl.ds(self.m1 * 64, 64)]
        self.sum1[s] = (own + a[0, s]) + (a[1, s] + a[2, s])
        for copy in self.two:
            copy.start()

    def reduce2(self):
        for copy in self.two:
            copy.wait_recv()
        a, s = self.arrived2, self.slabs
        own = self.sum1[s, pl.ds(self.m2 * 16, 16)]
        self.arrived3[self.m3, s] = (own + a[0, s]) + (a[1, s] + a[2, s])
        for copy in self.three:
            copy.start()

    def reduce3(self):
        for copy in self.three:
            copy.wait()
        a, s = self.arrived3, self.slabs
        self.full[pl.ds(self.base, self.n), pl.ds(self.m1 * 64 + self.m2 * 16, 16)] = (
            a[0, s] + a[1, s]
        ) + (a[2, s] + a[3, s])
        for copy in self.four:
            copy.start()

    def gather(self):
        for copy in self.four:
            copy.wait_recv()
        for copy in self.five:
            copy.start()

    def across(self):
        for copy in self.five:
            copy.wait_recv()
        self.six.start()

    def finish(self):
        self.six.wait()
        for copy in self.one + self.two + self.four + self.five:
            copy.wait_send()


def kernel(
    w_hbm, x_hbm, c_hbm, rb_hbm, cb_hbm,
    w, ph, pw, pth, ptw, xcat, xth, xtw, cols, pf,
    cp, csib, carr, cfull, ccat,
    ip, iarr1, ihalf, iarr2, imf,
    gp, gsib, garr, gfull, inv, vcat, th, tw, gh, gw,
    rb, dp, dsib, darr1, dsum1, darr2, dsum2, darr3, df,
    local_sem, send_sem, recv_sem,
):
    place = Place()
    c = place.at["c"]
    loads = [
        pltpu.make_async_copy(
            c_hbm.at[pl.ds(256 * t, 256), pl.ds(128 * s, 128)], df.at[8 * s + t],
            local_sem.at[11 + 8 * s + t],
        )
        for s in range(2)
        for t in range(8)
    ]
    order = [lax.rem(2 * (1 - c) + s, 4) for s in range(4)]
    wloads = [
        pltpu.make_async_copy(w_hbm.at[order[s]], w.at[order[s]], local_sem.at[2 + s])
        for s in range(4)
    ]
    xloads = [
        pltpu.make_async_copy(x_hbm.at[:, pl.ds(128 * q, 128)], imf.at[q], local_sem.at[6 + q])
        for q in range(4)
    ]
    for load in loads + wloads[:1]:
        load.start()

    barrier = pltpu.get_barrier_semaphore()
    pl.semaphore_signal(barrier, inc=1, device_id=place.peer("c", 1), device_id_type=MESH)
    for axis in ("x", "y", "z"):
        for d in (1, 2, 3):
            pl.semaphore_signal(barrier, inc=1, device_id=place.peer(axis, d), device_id_type=MESH)

    sender = Sender(place, send_sem, recv_sem)

    for n, load in enumerate(loads):
        load.wait()
        s, t = n // 8, n % 8
        cols[256 * t : 256 * t + 256, 128 * s : 128 * s + 128] = df[n].astype(BF16)
        if n == 11:
            wloads[1].start()
    for load in xloads:
        load.start()

    def row_sum(q):
        return RowSum(sender, 1024, cp.at[q], csib.at[q], carr.at[q], cfull.at[q])

    A = [row_sum(q) for q in range(4)]
    for s in range(4):
        e = order[s]
        wloads[s].wait()
        if s < 2:
            wloads[s + 2].start()
        at = pl.ds(pl.multiple_of(e * 256, 256), 256)

        def project(i, carry, e=e, at=at):
            r = pl.ds(pl.multiple_of(i * 448, 64), 448)
            value = dot(w[e, r, :], cols[...], 1, 0)
            pf[r, :] = value
            h, lo = split(value)
            ph[r, at] = h
            pw[r, at] = lo
            return carry

        lax.fori_loop(0, 2, project, 0)
        h, lo = split(pf[...].T)
        pth[at, :] = h
        ptw[at, :] = lo
        if s == 0:
            for q, load in enumerate(xloads):
                load.wait()
                h, lo = split(imf[q])
                xcat[q, :, :128] = h
                xcat[q, :, 128:] = lo
        if s % 2 == 0:
            continue
        pair = pl.ds(pl.multiple_of((1 - c if s == 1 else c) * 512, 512), 512)
        for q in range(0, 4, 2):
            right = jnp.concatenate([xcat[q, :, :128], xcat[q + 1, :, :128]], axis=1)
            low = dot(ptw[pair, :], right, 1, 0)
            for t in range(2):
                wide = dot(pth[pair, :], xcat[q + t], 1, 0)
                cp[q + t, pair, :] = wide[:, :128] + (
                    wide[:, 128:] + low[:, 128 * t : 128 * t + 128]
                )
        if s == 1:
            pl.semaphore_wait(barrier, 10)
            for one in A:
                one.start()

    def plane_sum(q):
        refs = (ip.at[q], iarr1.at[q], ihalf.at[q], iarr2.at[q], imf.at[q])
        return Pair(
            PlaneSum(sender, "x", "y", 0, 512, *refs), PlaneSum(sender, "y", "x", 512, 384, *refs)
        )

    B = [plane_sum(q) for q in range(4)]

    def image(q):
        h, lo = split(cfull[q])
        ccat[:, :128] = h
        ccat[:, 128:] = lo

        def body(i, carry):
            r = pl.ds(pl.multiple_of(i * 448, 64), 448)
            ip[q, r, :] = dot3n(ph[r, :], pw[r, :], ccat, 1, 0)
            return carry

        lax.fori_loop(0, 2, body, 0)
        B[q].start()

    C, G = [], []

    def gram(q):
        h, lo = split(imf[q])
        xcat[q, :, :128] = h
        xcat[q, :, 128:] = lo
        h, lo = split(imf[q].T)
        r = slice(128 * q, 128 * q + 128)
        xth[r, :] = h
        xtw[r, :] = lo
        n = 128 * (q + 1)
        at, half, part = 64 * q * (q + 1), 32 * q * (q + 1), 8 * q * (q + 1)
        own = gp.at[pl.ds(at, n)]
        own[...] = dot3n(xth[0:n, :], xtw[0:n, :], xcat.at[q], 1, 0)
        C.append(
            RowSum(
                sender, n, own, gsib.at[pl.ds(half, n // 2)],
                garr.at[:, pl.ds(part, n // 8)], gfull.at[pl.ds(at, n)],
            )
        )
        C[q].start()

    def under(q):
        def body(i, carry):
            r = pl.ds(pl.multiple_of(i * 512, 512), 512)
            cp[q, r, :] = dot3n(pth[r, :], ptw[r, :], xcat.at[q], 1, 0)
            return carry

        lax.fori_loop(0, 2, body, 0)
        G.append(row_sum(q))
        G[q].start()

    def factor(q, hooks={}):
        factor_step(q, C[q].full, inv, hooks)

    def basis(q):
        n = 128 * (q + 1)
        h, lo = split(inv[n - 128 : n, 0:n] * math.sqrt(D))
        vcat[0:128, 0:n] = h
        vcat[128:256, 0:n] = lo
        high = jnp.concatenate([xcat[p, :, :128] for p in range(q + 1)], axis=1)
        low = jnp.concatenate([xcat[p, :, 128:] for p in range(q + 1)], axis=1)
        value = dot3n(high, low, vcat.at[:, 0:n], 1, 1)
        rb[q] = value
        h, lo = split(value)
        ph[:, n - 128 : n] = h
        ph[:, 384 + n : 512 + n] = lo
        store = pltpu.make_async_copy(
            rb.at[q], rb_hbm.at[:, pl.ds(128 * q, 128)], local_sem.at[27 + q]
        )
        store.start()
        stores.append(store)

    def core_two(q):
        n = 128 * (q + 1)
        h, lo = split(cfull[q])
        gh[:, n - 128 : n] = h
        gw[:, n - 128 : n] = lo
        h, lo = split(inv[n - 128 : n, 0:n] * math.sqrt(D))
        vcat[0:128, 0:n] = h
        vcat[128:256, 0:n] = lo
        h, lo = split(dot3n(gh[:, 0:n], gw[:, 0:n], vcat.at[:, 0:n], 1, 1))
        th[:, n - 128 : n] = h
        tw[:, n - 128 : n] = lo

    def steps(*calls):
        def run():
            for call in calls:
                call()

        return run

    inv[...] = jnp.zeros_like(inv)
    stores = []
    A[0].scatter()
    A[1].scatter()
    A[0].reduce()
    A[1].reduce()
    A[2].scatter()
    A[3].scatter()
    A[0].forward()
    A[0].finish()
    image(0)
    A[1].forward()
    A[1].finish()
    image(1)
    A[2].reduce()
    B[0].reduce1()
    A[3].reduce()
    A[2].forward()
    B[1].reduce1()
    B[0].reduce2()
    A[2].finish()
    image(2)
    B[0].gather()
    B[1].reduce2()
    A[3].forward()
    A[3].finish()
    image(3)
    B[2].reduce1()
    B[0].finish()
    gram(0)
    C[0].scatter()
    under(0)
    B[1].gather()
    B[3].reduce1()
    B[2].reduce2()
    C[0].reduce()
    C[0].forward()
    C[0].finish()
    factor(0, {
        4: steps(
            lambda: G[0].scatter(),
            lambda: B[3].reduce2(),
            lambda: B[2].gather(),
        ),
    })
    G[0].reduce()
    B[3].gather()
    B[1].finish()
    gram(1)
    under(1)
    C[1].scatter()
    B[2].finish()
    gram(2)
    under(2)
    C[2].scatter()
    C[1].reduce()
    B[3].finish()
    gram(3)
    under(3)
    C[3].scatter()
    C[2].reduce()
    G[1].scatter()
    C[1].forward()
    C[1].finish()
    factor(1, {
        4: steps(
            lambda: G[3].scatter(),
        ),
        12: steps(
            lambda: C[3].reduce(),
            lambda: C[2].forward(),
            lambda: G[1].reduce(),
        ),
    })
    C[2].finish()
    factor(2, {
        4: steps(
            lambda: G[3].reduce(),
            lambda: G[2].scatter(),
            lambda: basis(1),
            lambda: C[3].forward(),
        ),
    })
    basis(2)
    C[3].finish()
    factor(3, {
        12: steps(
            lambda: G[1].forward(),
            lambda: G[2].reduce(),
        ),
    })
    basis(3)
    G[0].forward()
    G[0].finish()
    core_two(0)
    G[1].finish()
    core_two(1)
    G[2].forward()
    G[3].forward()
    basis(0)
    G[2].finish()
    core_two(2)
    G[3].finish()
    core_two(3)

    def back(i, carry):
        r = pl.ds(pl.multiple_of(i * 256, 256), 256)
        pth[r, :] = dot3(th[r, :], tw[r, :], ph[:, 0:512], ph[:, 512:1024], 1, 1).astype(BF16)
        return carry

    lax.fori_loop(0, 4, back, 0)

    def column_image(i, carry, half):
        f = pl.multiple_of(half * 1024 + i * 256, 256)
        value = dot(pth[0:256, :], w[0, :, pl.ds(f, 256)], 1, 0)
        for e in range(1, 4):
            value = value + dot(pth[256 * e : 256 * e + 256, :], w[e, :, pl.ds(f, 256)], 1, 0)
        s = half * 8 + i * 2
        dp[s] = value[:, :128]
        dp[s + 1] = value[:, 128:]
        return carry

    lax.fori_loop(0, 4, functools.partial(column_image, half=1 - c), 0)
    swap = sender.copy(dp.at[pl.ds((1 - c) * 8, 8)], dsib, "c", 1)
    swap.start()
    lax.fori_loop(0, 4, functools.partial(column_image, half=c), 0)
    groups = [("zxy", 0, 3), ("xyz", 3, 3), ("yzx", 6, 2)]
    cubes = [
        CubeSum(sender, axes, u0, n, dp, darr1, dsum1, darr2, dsum2, darr3, df)
        for axes, u0, n in groups
    ]
    swap.wait()
    for one, (axes, u0, n) in zip(cubes, groups):
        mine = pl.ds(c * 8 + u0, n)
        dp[mine] = dp[mine] + dsib[pl.ds(u0, n)]
        one.start()
    for step in ("reduce1", "reduce2", "reduce3", "gather", "across", "finish"):
        for one in cubes:
            getattr(one, step)()

    for s in range(8):
        h, lo = split(jnp.concatenate([df[2 * s], df[2 * s + 1]], axis=1))
        term = dot3(h, lo, h, lo, 1, 1)
        value = term if s == 0 else value + term
    gp[0:128, :] = value[0:128, 0:128]
    gp[128:384, :] = value[:, 128:256]
    factor_step(0, gp.at[0:128], inv)
    factor_step(1, gp.at[128:384], inv)
    h, lo = split(inv[0:256, 0:256] * math.sqrt(F))
    vcat[:, 0:256] = h
    vcat[:, 256:512] = lo
    for t in range(8):
        h, lo = split(jnp.concatenate([df[2 * t].T, df[2 * t + 1].T], axis=0))
        value = dot3(h, lo, vcat[:, 0:256], vcat[:, 256:512], 1, 1)
        for g in range(2):
            dp[8 * g + t] = value[:, 128 * g : 128 * g + 128]
            store = pltpu.make_async_copy(
                dp.at[8 * g + t],
                cb_hbm.at[pl.ds(256 * t, 256), pl.ds(128 * g, 128)],
                local_sem.at[11 + 2 * t + g],
            )
            store.start()
            stores.append(store)
    for store in stores:
        store.wait()


COPIES = 288


def shards(weights, prev_rows, prev_cols):
    vm = pltpu.VMEM
    return pl.pallas_call(
        kernel,
        name="orthogonal_step",
        out_shape=(
            jax.ShapeDtypeStruct((ROWS, R1), F32),
            jax.ShapeDtypeStruct((F, R2), F32),
        ),
        in_specs=[pl.BlockSpec(memory_space=pl.ANY)] * 3,
        out_specs=[pl.BlockSpec(memory_space=pl.ANY)] * 2,
        scratch_shapes=[
            vm((LOCAL, ROWS, F), BF16),
            vm((ROWS, 1024), BF16), vm((ROWS, 1024), BF16),
            vm((1024, ROWS), BF16), vm((1024, ROWS), BF16),
            vm((4, ROWS, 256), BF16), vm((R1, ROWS), BF16), vm((R1, ROWS), BF16),
            vm((F, R2), BF16), vm((ROWS, R2), F32),
            vm((4, 1024, 128), F32), vm((4, 512, 128), F32), vm((4, 3, 128, 128), F32),
            vm((4, 1024, 128), F32), vm((1024, 256), BF16),
            vm((4, ROWS, 128), F32), vm((4, 3, 224, 128), F32), vm((4, 224, 128), F32),
            vm((4, 3, 56, 128), F32), vm((4, ROWS, 128), F32),
            vm((1280, 128), F32), vm((640, 128), F32), vm((3, 160, 128), F32), vm((1280, 128), F32),
            vm((R1, R1), F32), vm((256, R1), BF16),
            vm((1024, R1), BF16), vm((1024, R1), BF16), vm((1024, R1), BF16), vm((1024, R1), BF16),
            vm((4, ROWS, 128), F32),
            vm((16, 256, 128), F32), vm((8, 256, 128), F32), vm((3, 8, 64, 128), F32),
            vm((8, 64, 128), F32), vm((3, 8, 16, 128), F32), vm((8, 16, 128), F32),
            vm((4, 8, 16, 128), F32), vm((16, 256, 128), F32),
            pltpu.SemaphoreType.DMA((32,)),
            pltpu.SemaphoreType.DMA((COPIES,)),
            pltpu.SemaphoreType.DMA((COPIES,)),
        ],
        compiler_params=pltpu.CompilerParams(
            collective_id=0, has_side_effects=True, vmem_limit_bytes=62 * 2**20
        ),
        cost_estimate=pl.CostEstimate(flops=12 * 10**9, bytes_accessed=25 * 10**6, transcendentals=0),
    )(weights, prev_rows, prev_cols)


def solution(mesh):
    placed = (P("expert", "row", None), P("row", None), P())
    return jax.shard_map(
        shards, mesh=mesh, in_specs=placed, out_specs=(P("row", None), P()), check_vma=False
    )
```
